256 devices in a mesh: prompt: 16 (over y_lo, z), slab: 16 (over y_hi, x, core).
Axes of the slice: x: 4, y: 4 (y_hi: 2, y_lo: 2; y = y_hi * 2 + y_lo), z: 8, core: 2. Of those that a mesh axis runs over, the one named last changes fastest.
Arguments:
- queries: bfloat16 [16, 8192, 1536], P('prompt', 'slab'), may hold values from -8 to 8
- key_value: bfloat16 [2, 16, 8192, 1536], P(None, 'prompt', 'slab'), may hold values from -6 to 6
- text_kv: bfloat16 [2, 16, 256, 1536], P(None, 'prompt', 'slab'), may hold values from -9 to 9
- residual: bfloat16 [16, 8192, 3072], P('prompt', 'slab'), may hold values from -1.5 to 1.5
- gate: float32 [16, 3072], P('prompt'), may hold values from 0.5 to 2
- bias: float32 [3072], replicated, may hold values from -1.2 to 1.2
- proj_weight: bfloat16 [1536, 3072], P('prompt'), may hold values from -0.15625 to 0.15625
- block_list: int32 [64, 8], P('slab'), may hold values from 0 to 63, as said below
- block_count: int32 [64], P('slab'), may hold values from 2 to 8, as said below
Outputs:
- output: bfloat16 [16, 8192, 3072], P('prompt', 'slab')
The draws below stay inside these ranges and needn't reach their ends.
Inputs may be any that keep to these rules, and one draw needn't show every extreme that they name: `block_list`: entry 0 of row t is t itself; entries 1 to block_count[t] - 1 are distinct tiles other than t that lie in the slab of t or in one of the two slabs beside it (tile g lies in slab g // 4); the remaining entries repeat t. `block_count`: the first tile of every slab uses all 8 entries.
All inputs are finite; a program needn't handle non-finite values.
Results may differ from the reference program's by a relative error of at most 0.0048.
Values may be sent and summed in bfloat16 or wider, within the bound.
A program may use at most 128 MiB of HBM per device.

```python
import jax
import jax.numpy as jnp
from jax import lax

D = 3072
HEADS = 12
HDIM = 128
TXT = 256
TILE = 128
TPD = 4
HD = 1536
NB = 8
TILES = 64
TOKENS = 8192
CLIPS = 16
N_SLAB = 16


def draw_queries(key, part):
    shape = (CLIPS, TOKENS, HD)
    background = jnp.clip(2.0 * jax.random.normal(jax.random.fold_in(key, 1), shape, jnp.float32), -8.0, 8.0)
    return background.astype(jnp.bfloat16)


def draw_key_value(key, part):
    shape = (2, CLIPS, TOKENS, HD)
    background = jnp.clip(jax.random.normal(jax.random.fold_in(key, 2), shape, jnp.float32), -6.0, 6.0)
    return background.astype(jnp.bfloat16)


def tile_lists(key):
    list_key = jax.random.fold_in(key, 11)
    key_perm, key_count = jax.random.split(list_key)
    spread = 3 * TPD
    shuffled = jax.vmap(lambda subkey: jax.random.permutation(subkey, spread))(jax.random.split(key_perm, TILES))
    own_tile = jnp.arange(TILES, dtype=jnp.int32)
    candidate = (own_tile[:, None] // TPD - 1) * TPD + jnp.arange(spread, dtype=jnp.int32)[None, :]
    usable = (candidate >= 0) & (candidate < TILES) & (candidate != own_tile[:, None])
    ranking = jnp.where(usable, shuffled, shuffled + spread)
    picked_order = jnp.argsort(ranking, axis=1, stable=True)[:, :NB - 1]
    picked = jnp.take_along_axis(candidate, picked_order, axis=1)
    tile_list = jnp.concatenate([own_tile[:, None], picked], 1)
    counts = jax.random.randint(key_count, (TILES,), 2, NB + 1)
    counts = jnp.where(own_tile % TPD == 0, NB, counts)
    used = jnp.arange(NB)[None, :] < counts[:, None]
    tile_list = jnp.where(used, tile_list, own_tile[:, None])
    return (tile_list.astype(jnp.int32), counts.astype(jnp.int32))


def draw_block_list(key, part):
    return tile_lists(key)[0]


def draw_block_count(key, part):
    return tile_lists(key)[1]


def steps_of(own_key, shape, cuts, least, top_value):
    loudness, own = 1.0, jax.random.fold_in(own_key, 6)
    for axis_at, shards_of in cuts:
        steps = jnp.exp(jax.random.uniform(jax.random.fold_in(own, axis_at), (shards_of,), jnp.float32, least / len(cuts), top_value / len(cuts)))
        loudness = loudness * jnp.repeat(steps, shape[axis_at] // shards_of).reshape([-1 if axis == axis_at else 1 for axis in range(len(shape))])
    return loudness


def scatter_about(stream_key, shape, scale, bound, cuts=(), kind=jnp.bfloat16):
    values = jax.random.normal(stream_key, shape, jnp.float32) * scale
    if len(cuts) > 0:
        values = steps_of(stream_key, shape, cuts, -0.22, 0.18) * values
    return jnp.clip(values, min=-bound, max=bound).astype(kind)


def setup_inputs(seed: int = 0) -> dict:
    streams_of = jax.random.split(jax.random.key(seed), 10)
    queries = draw_queries(jax.random.fold_in(streams_of[9], 71), 0)
    key_value = draw_key_value(jax.random.fold_in(streams_of[9], 71), 0)
    text_kv = scatter_about(streams_of[2], (2, CLIPS, TXT, HD), 1.5, 9.0, ((1, 16), (2, 16)))
    residual = scatter_about(streams_of[3], (CLIPS, TOKENS, D), 0.25, 1.5, ((0, 16), (1, 16)))
    gate = jnp.clip(0.5 + 1.5 * jax.random.uniform(streams_of[4], (CLIPS, D), jnp.float32) ** steps_of(streams_of[4], (CLIPS, D), ((0, 16),), -0.2, 0.2), 0.5, 2.0)
    bias = scatter_about(streams_of[5], (D,), 0.2, 1.2, (), jnp.float32)
    proj_weight = scatter_about(streams_of[6], (HD, D), HD ** -0.5, 0.15625, ((0, 16),))
    block_list = draw_block_list(jax.random.fold_in(streams_of[9], 71), 0)
    block_count = draw_block_count(jax.random.fold_in(streams_of[9], 71), 0)
    return dict(queries=queries, key_value=key_value, text_kv=text_kv, residual=residual, gate=gate, bias=bias, proj_weight=proj_weight, block_list=block_list, block_count=block_count)


masked_score = -1e30


def membership(block_list, block_count):
    all_tiles = jnp.arange(TILES, dtype=jnp.int32)
    first_tile = (all_tiles // TPD - 1) * TPD
    candidate = first_tile[:, None] + jnp.arange(3 * TPD, dtype=jnp.int32)[None, :]
    usable = jnp.arange(NB, dtype=jnp.int32)[None, :] < block_count[:, None]
    matches = (block_list[:, :, None] == candidate[:, None, :]) & usable[:, :, None]
    return jnp.any(matches, axis=1)


def attend(query_rows, video_keys, video_values, text_keys, text_values, member):
    row_count = query_rows.shape[0]
    keys_all = jnp.concatenate([video_keys, text_keys], 0).astype(jnp.float32)
    values_all = jnp.concatenate([video_values, text_values], 0).astype(jnp.float32)
    query_heads = query_rows.astype(jnp.float32).reshape(row_count, HEADS, HDIM)
    key_heads = keys_all.reshape(-1, HEADS, HDIM)
    value_heads = values_all.reshape(-1, HEADS, HDIM)
    scores = jnp.einsum("qhd,khd->hqk", query_heads, key_heads) * (HDIM ** -0.5)
    tile_mask = jnp.repeat(jnp.repeat(member, TILE, axis=0), TILE, axis=1)
    allowed = jnp.concatenate([tile_mask, jnp.ones((row_count, TXT), dtype=bool)], 1)
    scores = jnp.where(allowed[None], scores, masked_score)
    row_max = jnp.max(scores, axis=2, keepdims=True)
    exponent = jnp.where(allowed[None], jnp.exp(scores - row_max), 0.0)
    row_total = jnp.sum(exponent, axis=2)
    weights = lax.optimization_barrier(exponent.astype(jnp.bfloat16)).astype(jnp.float32)
    weighted = jnp.einsum("hqk,khd->qhd", weights, value_heads)
    weighted = weighted / jnp.transpose(row_total)[:, :, None]
    return weighted.reshape(row_count, HEADS * HDIM).astype(jnp.bfloat16)


def reference(queries, key_value, text_kv, residual, gate, bias, proj_weight, block_list, block_count):
    member = membership(block_list, block_count)
    slab_tokens = TPD * TILE

    def one_clip(clip_index):
        query_clip = queries[clip_index]
        keys_pad = jnp.pad(key_value[0, clip_index], ((slab_tokens, slab_tokens), (0, 0)))
        values_pad = jnp.pad(key_value[1, clip_index], ((slab_tokens, slab_tokens), (0, 0)))
        text_keys = text_kv[0, clip_index]
        text_values = text_kv[1, clip_index]

        def one_slab(slab_index):
            offset = (slab_index * slab_tokens).astype(jnp.int32)
            query_rows = lax.dynamic_slice_in_dim(query_clip, offset, slab_tokens, 0)
            video_keys = lax.dynamic_slice_in_dim(keys_pad, offset, 3 * slab_tokens, 0)
            video_values = lax.dynamic_slice_in_dim(values_pad, offset, 3 * slab_tokens, 0)
            tile_member = lax.dynamic_slice_in_dim(member, (slab_index * TPD).astype(jnp.int32), TPD, 0)
            return attend(query_rows, video_keys, video_values, text_keys, text_values, tile_member)

        attended = lax.map(one_slab, jnp.arange(N_SLAB, dtype=jnp.int32)).reshape(TOKENS, HEADS * HDIM)
        projected = jnp.dot(attended, proj_weight, preferred_element_type=jnp.float32)
        result = residual[clip_index].astype(jnp.float32) + gate[clip_index][None, :] * (projected + bias[None, :])
        return result.astype(jnp.bfloat16)

    return lax.map(one_clip, jnp.arange(CLIPS, dtype=jnp.int32))
```

```python
import functools

import jax
import jax.numpy as jnp
from jax import lax
from jax.experimental import pallas as pl
from jax.experimental.pallas import tpu as pltpu
from jax.sharding import PartitionSpec as P

MESH = pl.DeviceIdType.MESH
HEADS = 12
HDIM = 128
TILE = 128
TPD = 4
NB = 8
ROWS = 512
HD = 1536
D = 3072
TXT = 256
SHARD = 96
HALF = 48
BLOCK = 256
OUT_COLS = 512
SIDE = 768
PART = 1536
masked_score = -1e30
EXP2_SCALE = HDIM**-0.5 * 1.4426950408889634
CONTRACT_LAST = (((1,), (1,)), ((), ()))


def attend_head(head, q, kvb, txt, mask, att):
    col = pl.ds(pl.multiple_of(head * HDIM, HDIM), HDIM)
    for start in range(0, ROWS, BLOCK):
        rows = q[pl.ds(start, BLOCK), col]
        parts = []
        for source in range(3):
            scores = lax.dot_general(
                rows, kvb[source, 0, :, col], CONTRACT_LAST, preferred_element_type=jnp.float32
            )
            tiles = []
            for t in range(BLOCK // TILE):
                at = start // TILE + t
                tiles.append(
                    scores[t * TILE : (t + 1) * TILE]
                    + mask[at : at + 1, source * ROWS : (source + 1) * ROWS]
                )
            parts.append(jnp.concatenate(tiles, 0))
        parts.append(
            lax.dot_general(rows, txt[0, :, col], CONTRACT_LAST, preferred_element_type=jnp.float32)
        )
        largest = functools.reduce(
            jnp.maximum, [jnp.max(part, axis=1, keepdims=True) for part in parts]
        )
        shift = largest * EXP2_SCALE
        total, weighted = None, None
        for i, part in enumerate(parts):
            weights = jnp.exp2(part * EXP2_SCALE - shift)
            part_total = jnp.sum(weights, axis=1, keepdims=True)
            values = kvb[i, 1, :, col] if i < 3 else txt[1, :, col]
            part_weighted = jnp.dot(
                weights.astype(jnp.bfloat16), values, preferred_element_type=jnp.float32
            )
            total = part_total if i == 0 else total + part_total
            weighted = part_weighted if i == 0 else weighted + part_weighted
        att[pl.ds(start, BLOCK), col] = (weighted / total).astype(jnp.bfloat16)


def kernel(
    q_hbm,
    kv_hbm,
    t_hbm,
    res_hbm,
    gate,
    bias,
    w_hbm,
    block_list,
    block_count,
    out_hbm,
    q,
    kvb,
    txt,
    wfull,
    mask,
    att,
    acc,
    res,
    local_sem,
    out_sem,
    kvx_send,
    kvx_recv,
    kvc_send,
    kvc_recv,
    text_send,
    text_recv,
    wz_send,
    wz_recv,
    wy_send,
    wy_recv,
    wp_send,
    wp_recv,
):
    p, s = lax.axis_index("prompt"), lax.axis_index("slab")
    y_lo, z = p // 8, p % 8
    y_hi, x, c = s // 8, (s % 8) // 2, s % 2
    y = y_hi * 2 + y_lo

    def device(x, y, z, c):
        return {"prompt": (y % 2) * 8 + z, "slab": (y // 2) * 8 + x * 2 + c}

    partner = device(x, y, z, 1 - c)
    far = s - 1 + 2 * c
    has_far = (far >= 0) & (far < 16)
    far_device = {"prompt": p, "slab": jnp.clip(far, 0, 15)}
    along = 1 - 2 * c
    z_of = lambda k: lax.rem(z + along * k + 8, 8)
    z_next, z_prev = device(x, y, z_of(1), c), device(x, y, z_of(-1), c)
    y_next, y_prev = device(x, lax.rem(y + 1, 4), z, c), device(x, lax.rem(y + 3, 4), z, c)
    both_y = ((x == 0) & (y_hi == 1)) | ((x == 3) & (y_hi == 0))
    inner = (x == 1) | (x == 2)
    up_y, down_y = both_y | (inner & (y_lo == 0)), both_y | (inner & (y_lo == 1))
    head_of = lambda i: lax.rem(i + y_lo * 6, HEADS)
    chips = [(dx, dy) for dy in (0, 2) for dx in range(4) if dx or dy]
    clip_chips = [
        device(lax.rem(x + dx, 4), lax.rem(y + dy, 4), z, c) for dx, dy in chips
    ]
    middle = (s == 7) | (s == 8)

    barrier = pltpu.get_barrier_semaphore()
    fixed = [partner, z_next, z_prev, y_next, y_prev] + clip_chips
    for target in fixed:
        pl.semaphore_signal(barrier, inc=1, device_id=target, device_id_type=MESH)

    @pl.when(has_far)
    def _():
        pl.semaphore_signal(barrier, inc=1, device_id=far_device, device_id_type=MESH)

    text_own = pl.ds(pl.multiple_of(((c * 2 + y_hi) * 4 + x) * 16, 16), 16)
    copy_q = pltpu.make_async_copy(q_hbm, q, local_sem.at[0])
    copy_kv = pltpu.make_async_copy(kv_hbm, kvb.at[0], local_sem.at[1])
    copy_text = pltpu.make_async_copy(t_hbm, txt.at[:, text_own, :], local_sem.at[2])
    copy_w = pltpu.make_async_copy(
        w_hbm, wfull.at[pl.ds(pl.multiple_of(p * SHARD, SHARD), SHARD)], local_sem.at[3]
    )
    copy_res = pltpu.make_async_copy(res_hbm, res, local_sem.at[4])
    copy_edge = pltpu.make_async_copy(kv_hbm, kvb.at[2], local_sem.at[5])
    for copy in (copy_text, copy_kv, copy_q, copy_w, copy_res):
        copy.start()

    @pl.when(jnp.logical_not(has_far))
    def _():
        copy_edge.start()

    lane = lax.broadcasted_iota(jnp.int32, (1, 3 * ROWS), 1)
    slab_of = jnp.where(lane < ROWS, s, jnp.where(lane < 2 * ROWS, s + 1 - 2 * c, far))
    tile_of = slab_of * TPD + lax.rem(lane, ROWS) // TILE
    for t in range(TPD):
        member = None
        for n in range(NB):
            listed = jnp.where(n < block_count[t], block_list[t, n], -1000)
            match = tile_of == listed
            member = match if n == 0 else member | match
        mask[t : t + 1, :] = jnp.where(member, 0.0, masked_score)

    pl.semaphore_wait(barrier, len(fixed) + has_far.astype(jnp.int32))

    def remote(src, dst, send_sem, recv_sem, to):
        return pltpu.make_async_remote_copy(
            src_ref=src,
            dst_ref=dst,
            send_sem=send_sem,
            recv_sem=recv_sem,
            device_id=to,
            device_id_type=MESH,
        )

    text_half = pl.ds(pl.multiple_of(c * 128, 128), 128)

    def text_out(i):
        return remote(
            t_hbm, txt.at[:, text_own, :], text_send.at[i], text_recv.at[i], clip_chips[i]
        )

    def text_partner():
        block = txt.at[:, text_half, :]
        return remote(block, block, text_send.at[7], text_recv.at[7], partner)

    def w_block(side, z_at, core, part):
        start = (side * 8 + z_at) * SHARD + core * HALF
        return wfull.at[pl.ds(pl.multiple_of(start, 16), HALF), pl.ds(part * PART, PART)]

    def w_own(part):
        return w_hbm.at[pl.ds(pl.multiple_of(c * HALF, 16), HALF), pl.ds(part * PART, PART)]

    sides, parts = (y_lo, y_lo, 1 - y_lo), (0, 1, 1)

    def w_z(stream, slot):
        offset = -slot if slot < 4 else slot - 4
        dst = w_block(sides[stream], z_of(offset), c, parts[stream])
        src = w_own(parts[stream]) if stream < 2 and offset == 0 else dst
        at = stream * 7 + slot
        return remote(src, dst, wz_send.at[at], wz_recv.at[at], z_next if slot < 4 else z_prev)

    def w_z_partner(stream, offset):
        block = w_block(sides[stream], z_of(offset), c, parts[stream])
        at = stream * 7 + (-offset - 1 if offset < 0 else 3 + offset)
        return remote(block, block, wp_send.at[at], wp_recv.at[at], partner)

    across_offsets = [0, 0, -1, 1, -2, 2, -3, 3, -4]

    def w_y(i, up):
        part = 1 if i == 0 else 0
        dst = w_block(y_lo, z_of(across_offsets[i]), c, part)
        src = w_own(part) if i < 2 else dst
        at = i if up else 9 + i
        return remote(src, dst, wy_send.at[at], wy_recv.at[i], y_next if up else y_prev)

    def w_y_partner(i):
        block = w_block(1 - y_lo, z_of(across_offsets[i]), c, 1 if i == 0 else 0)
        return remote(block, block, wp_send.at[21 + i], wp_recv.at[21 + i], partner)

    def send_y(i):
        pl.when(up_y)(lambda: w_y(i, True).start())
        pl.when(down_y)(lambda: w_y(i, False).start())

    def kv_cols(h):
        if isinstance(h, int):
            return pl.ds(h * HDIM, HDIM)
        return pl.ds(pl.multiple_of(h * HDIM, HDIM), HDIM)

    def kv_far(h):
        return remote(
            kv_hbm.at[:, :, kv_cols(h)],
            kvb.at[2, :, :, kv_cols(h)],
            kvx_send.at[h],
            kvx_recv.at[h],
            far_device,
        )

    def kv_near(h):
        return remote(
            kv_hbm.at[:, :, kv_cols(h)],
            kvb.at[1, :, :, kv_cols(h)],
            kvc_send.at[h],
            kvc_recv.at[h],
            partner,
        )

    def send_far():
        @pl.when(has_far)
        def _():
            for i in range(HEADS):
                kv_far(head_of(i)).start()

    for i in range(7):
        text_out(i).start()
    w_z(0, 0).start()
    w_z(0, 4).start()
    send_y(0)
    pl.when(jnp.logical_not(middle))(lambda: send_far())
    w_z(1, 0).start()
    w_z(1, 4).start()
    send_y(1)
    kv_near(head_of(0)).start()
    kv_near(head_of(1)).start()

    copy_text.wait()
    copy_kv.wait()
    copy_q.wait()
    copy_w.wait()
    copy_res.wait()

    @pl.when(jnp.logical_not(has_far))
    def _():
        copy_edge.wait()

    def text_first():
        for i in range(7):
            text_out(i).wait_recv()
        text_partner().start()
        pl.when(middle)(lambda: send_far())

    def ring(stream, d):
        w_z(stream, d - 1).wait_recv()
        if d < 4:
            w_z(stream, d).start()
        if stream == 0:
            send_y(2 * d)
        w_z_partner(stream, -d).start()
        if d < 4:
            w_z(stream, 3 + d).wait_recv()
            if d < 3:
                w_z(stream, 4 + d).start()
            if stream == 0:
                send_y(2 * d + 1)
            w_z_partner(stream, d).start()

    def across(*slots):
        for i in slots:
            w_y(i, True).wait_recv()
            if i == 0:
                w_z(2, 0).start()
                w_z(2, 4).start()
            w_y_partner(i).start()

    events = {
        0: [
            lambda: across(0),
            lambda: ring(0, 1),
            lambda: text_first(),
            lambda: ring(1, 1),
            lambda: ring(2, 1),
            lambda: text_partner().wait_recv(),
        ],
        1: [lambda: ring(0, 2), lambda: across(1, 2, 3)],
        2: [lambda: ring(1, 2)],
        4: [lambda: ring(2, 2)],
        5: [lambda: ring(0, 3), lambda: across(4, 5)],
        6: [lambda: ring(1, 3)],
        7: [lambda: ring(2, 3)],
        8: [lambda: ring(0, 4), lambda: across(6, 7)],
        9: [lambda: ring(1, 4)],
        10: [lambda: ring(2, 4), lambda: across(8)],
    }
    own_side = pl.ds(pl.multiple_of(y_lo * SIDE, SIDE), SIDE)
    other_side = pl.ds(pl.multiple_of((1 - y_lo) * SIDE, SIDE), SIDE)

    def project_own():
        for stream in range(2):
            for d in (-4, -3, -2, -1, 1, 2, 3):
                w_z_partner(stream, d).wait_recv()

        def column(j, _):
            cols = pl.ds(pl.multiple_of(j * OUT_COLS, OUT_COLS), OUT_COLS)
            acc[:, cols] = jnp.dot(
                att[:, own_side], wfull[own_side, cols], preferred_element_type=jnp.float32
            )
            return 0

        lax.fori_loop(0, D // OUT_COLS, column, 0)

    def step(h, _):
        for at, actions in events.items():

            @pl.when(h == at)
            def _():
                for action in actions:
                    action()

        @pl.when(h < HEADS - 2)
        def _():
            kv_near(head_of(h + 2)).start()

        head = head_of(h)
        kv_near(head).wait_recv()

        @pl.when(has_far)
        def _():
            kv_far(head).wait_recv()

        attend_head(head, q, kvb, txt, mask, att)

        @pl.when(h == 10)
        def _():
            project_own()

        return 0

    lax.fori_loop(0, HEADS, step, 0)
    for d in (-4, -3, -2, -1, 1, 2, 3):
        w_z_partner(2, d).wait_recv()
    for i in range(9):
        w_y_partner(i).wait_recv()

    def copy_out(j):
        cols = pl.ds(pl.multiple_of(j * OUT_COLS, OUT_COLS), OUT_COLS)
        return pltpu.make_async_copy(res.at[:, cols], out_hbm.at[:, cols], out_sem.at[j])

    def finish(j, _):
        cols = pl.ds(pl.multiple_of(j * OUT_COLS, OUT_COLS), OUT_COLS)
        projected = acc[:, cols] + jnp.dot(
            att[:, other_side], wfull[other_side, cols], preferred_element_type=jnp.float32
        )
        result = res[:, cols].astype(jnp.float32) + gate[:, cols] * (projected + bias[:, cols])
        res[:, cols] = result.astype(jnp.bfloat16)
        copy_out(j).start()
        return 0

    lax.fori_loop(0, D // OUT_COLS, finish, 0)

    for i in range(7):
        text_out(i).wait_send()
    text_partner().wait_send()
    for stream in range(3):
        for slot in range(7):
            w_z(stream, slot).wait_send()
        for d in (-4, -3, -2, -1, 1, 2, 3):
            w_z_partner(stream, d).wait_send()
    for i in range(9):
        w_y_partner(i).wait_send()

    @pl.when(up_y)
    def _():
        for i in range(9):
            w_y(i, True).wait_send()

    @pl.when(down_y)
    def _():
        for i in range(9):
            w_y(i, False).wait_send()


    def sent(h, _):
        kv_near(h).wait_send()

        @pl.when(has_far)
        def _():
            kv_far(h).wait_send()

        return 0

    lax.fori_loop(0, HEADS, sent, 0)
    lax.fori_loop(0, D // OUT_COLS, lambda j, _: (copy_out(j).wait(), 0)[1], 0)


def on_device(
    queries, key_value, text_kv, residual, gate, bias, proj_weight, block_list, block_count
):
    hbm = pl.BlockSpec(memory_space=pl.ANY)
    vmem = pl.BlockSpec(memory_space=pltpu.VMEM)
    smem = pl.BlockSpec(memory_space=pltpu.SMEM)
    dma = pltpu.SemaphoreType.DMA
    result = pl.pallas_call(
        kernel,
        out_shape=jax.ShapeDtypeStruct((ROWS, D), jnp.bfloat16),
        in_specs=[hbm, hbm, hbm, hbm, vmem, vmem, hbm, smem, smem],
        out_specs=hbm,
        scratch_shapes=[
            pltpu.VMEM((ROWS, HD), jnp.bfloat16),
            pltpu.VMEM((3, 2, ROWS, HD), jnp.bfloat16),
            pltpu.VMEM((2, TXT, HD), jnp.bfloat16),
            pltpu.VMEM((HD, D), jnp.bfloat16),
            pltpu.VMEM((TPD, 3 * ROWS), jnp.float32),
            pltpu.VMEM((ROWS, HD), jnp.bfloat16),
            pltpu.VMEM((ROWS, D), jnp.float32),
            pltpu.VMEM((ROWS, D), jnp.bfloat16),
            dma((6,)),
            dma((D // OUT_COLS,)),
            dma((HEADS,)),
            dma((HEADS,)),
            dma((HEADS,)),
            dma((HEADS,)),
            dma((8,)),
            dma((8,)),
            dma((21,)),
            dma((21,)),
            dma((18,)),
            dma((9,)),
            dma((30,)),
            dma((30,)),
        ],
        compiler_params=pltpu.CompilerParams(
            collective_id=0, has_side_effects=True, vmem_limit_bytes=60 * 2**20
        ),
    )(
        queries[0],
        key_value[:, 0],
        text_kv[:, 0],
        residual[0],
        gate,
        bias[None],
        proj_weight,
        block_list,
        block_count,
    )
    return result[None]


def solution(mesh):
    placed = (
        P("prompt", "slab", None),
        P(None, "prompt", "slab", None),
        P(None, "prompt", "slab", None),
        P("prompt", "slab", None),
        P("prompt", None),
        P(),
        P("prompt", None),
        P("slab", None),
        P("slab"),
    )
    return jax.shard_map(
        on_device, mesh=mesh, in_specs=placed, out_specs=P("prompt", "slab", None), check_vma=False
    )
```

```python
import functools

import jax
import jax.numpy as jnp
from jax import lax
from jax.experimental import pallas as pl
from jax.experimental.pallas import tpu as pltpu
from jax.sharding import PartitionSpec as P

MESH = pl.DeviceIdType.MESH
HEADS = 12
HDIM = 128
TILE = 128
TPD = 4
NB = 8
ROWS = 512
HD = 1536
D = 3072
TXT = 256
SHARD = 96
HALF = 48
BLOCK = 256
OUT_COLS = 512
BLOCKS = 3
SIDE = 768
PART = 1536
masked_score = -1e30
EXP2_SCALE = HDIM**-0.5 * 1.4426950408889634
CONTRACT_LAST = (((1,), (1,)), ((), ()))


def attend_head(head, q, kvb, txt, mask, att):
    col = pl.ds(pl.multiple_of(head * HDIM, HDIM), HDIM)
    for start in range(0, ROWS, BLOCK):
        rows = q[pl.ds(start, BLOCK), col]
        parts = []
        for source in range(3):
            scores = lax.dot_general(
                rows, kvb[source, 0, :, col], CONTRACT_LAST, preferred_element_type=jnp.float32
            )
            tiles = []
            for t in range(BLOCK // TILE):
                at = start // TILE + t
                tiles.append(
                    scores[t * TILE : (t + 1) * TILE]
                    + mask[at : at + 1, source * ROWS : (source + 1) * ROWS]
                )
            parts.append(jnp.concatenate(tiles, 0))
        parts.append(
            lax.dot_general(rows, txt[0, :, col], CONTRACT_LAST, preferred_element_type=jnp.float32)
        )
        largest = functools.reduce(
            jnp.maximum, [jnp.max(part, axis=1, keepdims=True) for part in parts]
        )
        shift = largest * EXP2_SCALE
        total, weighted = None, None
        for i, part in enumerate(parts):
            weights = jnp.exp2(part * EXP2_SCALE - shift)
            part_total = jnp.sum(weights, axis=1, keepdims=True)
            values = kvb[i, 1, :, col] if i < 3 else txt[1, :, col]
            part_weighted = jnp.dot(
                weights.astype(jnp.bfloat16), values, preferred_element_type=jnp.float32
            )
            total = part_total if i == 0 else total + part_total
            weighted = part_weighted if i == 0 else weighted + part_weighted
        att[pl.ds(start, BLOCK), col] = (weighted / total).astype(jnp.bfloat16)


def kernel(
    q_hbm,
    kv_hbm,
    t_hbm,
    res_hbm,
    gate,
    bias,
    w_hbm,
    block_list,
    block_count,
    out_hbm,
    q,
    kvb,
    txt,
    wfull,
    mask,
    att,
    acc,
    res,
    local_sem,
    out_sem,
    kvx_send,
    kvx_recv,
    kvc_send,
    kvc_recv,
    text_send,
    text_recv,
    wz_send,
    wz_recv,
    wy_send,
    wy_recv,
    wp_send,
    wp_recv,
):
    p, s = lax.axis_index("prompt"), lax.axis_index("slab")
    y_lo, z = p // 8, p % 8
    y_hi, x, c = s // 8, (s % 8) // 2, s % 2
    y = y_hi * 2 + y_lo

    def device(x, y, z, c):
        return {"prompt": (y % 2) * 8 + z, "slab": (y // 2) * 8 + x * 2 + c}

    partner = device(x, y, z, 1 - c)
    far = s - 1 + 2 * c
    has_far = (far >= 0) & (far < 16)
    far_device = {"prompt": p, "slab": jnp.clip(far, 0, 15)}
    along = 1 - 2 * c
    z_of = lambda k: lax.rem(z + along * k + 8, 8)
    z_next, z_prev = device(x, y, z_of(1), c), device(x, y, z_of(-1), c)
    y_next, y_prev = device(x, lax.rem(y + 1, 4), z, c), device(x, lax.rem(y + 3, 4), z, c)
    both_y = ((x == 0) & (y_hi == 1)) | ((x == 3) & (y_hi == 0))
    inner = (x == 1) | (x == 2)
    up_y, down_y = both_y | (inner & (y_lo == 0)), both_y | (inner & (y_lo == 1))
    head_of = lambda i: lax.rem(i + y_lo * 6, HEADS)
    y_far = device(x, lax.rem(y + 2, 4), z, c)
    x_others = [device(lax.rem(x + dx, 4), y, z, c) for dx in (1, 2, 3)]

    barrier = pltpu.get_barrier_semaphore()
    fixed = [partner, z_next, z_prev, y_next, y_prev, y_far] + x_others
    for target in fixed:
        pl.semaphore_signal(barrier, inc=1, device_id=target, device_id_type=MESH)

    @pl.when(has_far)
    def _():
        pl.semaphore_signal(barrier, inc=1, device_id=far_device, device_id_type=MESH)

    text_own = pl.ds(pl.multiple_of(((c * 2 + y_hi) * 4 + x) * 16, 16), 16)
    text_over = pl.ds(pl.multiple_of(((c * 2 + 1 - y_hi) * 4 + x) * 16, 16), 16)
    copy_q = pltpu.make_async_copy(q_hbm, q, local_sem.at[0])
    copy_kv = pltpu.make_async_copy(kv_hbm, kvb.at[0], local_sem.at[1])
    copy_text = pltpu.make_async_copy(t_hbm, txt.at[:, text_own, :], local_sem.at[2])
    copy_w = pltpu.make_async_copy(
        w_hbm, wfull.at[pl.ds(pl.multiple_of(p * SHARD, SHARD), SHARD)], local_sem.at[3]
    )
    copy_res = pltpu.make_async_copy(res_hbm, res, local_sem.at[4])
    copy_edge = pltpu.make_async_copy(kv_hbm, kvb.at[2], local_sem.at[5])
    for copy in (copy_text, copy_kv, copy_q, copy_w, copy_res):
        copy.start()

    @pl.when(jnp.logical_not(has_far))
    def _():
        copy_edge.start()

    lane = lax.broadcasted_iota(jnp.int32, (1, 3 * ROWS), 1)
    slab_of = jnp.where(lane < ROWS, s, jnp.where(lane < 2 * ROWS, s + 1 - 2 * c, far))
    tile_of = slab_of * TPD + lax.rem(lane, ROWS) // TILE
    for t in range(TPD):
        member = None
        for n in range(NB):
            listed = jnp.where(n < block_count[t], block_list[t, n], -1000)
            match = tile_of == listed
            member = match if n == 0 else member | match
        mask[t : t + 1, :] = jnp.where(member, 0.0, masked_score)

    pl.semaphore_wait(barrier, len(fixed) + has_far.astype(jnp.int32))

    def remote(src, dst, send_sem, recv_sem, to):
        return pltpu.make_async_remote_copy(
            src_ref=src,
            dst_ref=dst,
            send_sem=send_sem,
            recv_sem=recv_sem,
            device_id=to,
            device_id_type=MESH,
        )

    text_half = pl.ds(pl.multiple_of(c * 128, 128), 128)

    def text_y():
        return remote(t_hbm, txt.at[:, text_own, :], text_send.at[0], text_recv.at[0], y_far)

    def text_x(i, over):
        rows, at = (text_over, 4 + i) if over else (text_own, 1 + i)
        src = txt.at[:, rows, :] if over else t_hbm
        return remote(src, txt.at[:, rows, :], text_send.at[at], text_recv.at[at], x_others[i])

    def text_partner():
        block = txt.at[:, text_half, :]
        return remote(block, block, text_send.at[7], text_recv.at[7], partner)

    def w_block(side, z_at, core, part):
        start = (side * 8 + z_at) * SHARD + core * HALF
        return wfull.at[pl.ds(pl.multiple_of(start, 16), HALF), pl.ds(part * PART, PART)]

    def w_own(part):
        return w_hbm.at[pl.ds(pl.multiple_of(c * HALF, 16), HALF), pl.ds(part * PART, PART)]

    sides, parts = (y_lo, y_lo, 1 - y_lo), (0, 1, 1)

    def w_z(stream, slot):
        offset = -slot if slot < 4 else slot - 4
        dst = w_block(sides[stream], z_of(offset), c, parts[stream])
        src = w_own(parts[stream]) if stream < 2 and offset == 0 else dst
        at = stream * 7 + slot
        return remote(src, dst, wz_send.at[at], wz_recv.at[at], z_next if slot < 4 else z_prev)

    def w_z_partner(stream, offset):
        block = w_block(sides[stream], z_of(offset), c, parts[stream])
        at = stream * 7 + (-offset - 1 if offset < 0 else 3 + offset)
        return remote(block, block, wp_send.at[at], wp_recv.at[at], partner)

    across_offsets = [0, 0, -1, 1, -2, 2, -3, 3, -4]

    def w_y(i, up):
        part = 1 if i == 0 else 0
        dst = w_block(y_lo, z_of(across_offsets[i]), c, part)
        src = w_own(part) if i < 2 else dst
        at = i if up else 9 + i
        return remote(src, dst, wy_send.at[at], wy_recv.at[i], y_next if up else y_prev)

    def w_y_partner(i):
        block = w_block(1 - y_lo, z_of(across_offsets[i]), c, 1 if i == 0 else 0)
        return remote(block, block, wp_send.at[21 + i], wp_recv.at[21 + i], partner)

    def send_y(i):
        pl.when(up_y)(lambda: w_y(i, True).start())
        pl.when(down_y)(lambda: w_y(i, False).start())

    def kv_cols(h):
        if isinstance(h, int):
            return pl.ds(h * HDIM, HDIM)
        return pl.ds(pl.multiple_of(h * HDIM, HDIM), HDIM)

    def kv_far(h):
        return remote(
            kv_hbm.at[:, :, kv_cols(h)],
            kvb.at[2, :, :, kv_cols(h)],
            kvx_send.at[h],
            kvx_recv.at[h],
            far_device,
        )

    def kv_near(h):
        return remote(
            kv_hbm.at[:, :, kv_cols(h)],
            kvb.at[1, :, :, kv_cols(h)],
            kvc_send.at[h],
            kvc_recv.at[h],
            partner,
        )

    def send_far():
        @pl.when(has_far)
        def _():
            for i in range(HEADS):
                kv_far(head_of(i)).start()

    text_y().start()
    w_z(0, 0).start()
    w_z(0, 4).start()
    send_y(0)
    for i in range(3):
        text_x(i, False).start()
    w_z(1, 0).start()
    w_z(1, 4).start()
    send_y(1)
    kv_near(head_of(0)).start()
    kv_near(head_of(1)).start()

    copy_text.wait()
    copy_kv.wait()
    copy_q.wait()
    copy_w.wait()
    copy_res.wait()

    @pl.when(jnp.logical_not(has_far))
    def _():
        copy_edge.wait()

    def text_first():
        text_y().wait_recv()
        for i in range(3):
            text_x(i, True).start()
        send_far()

    def text_second():
        for i in range(3):
            text_x(i, False).wait_recv()
            text_x(i, True).wait_recv()
        text_partner().start()

    def ring(stream, d):
        w_z(stream, d - 1).wait_recv()
        if d < 4:
            w_z(stream, d).start()
        if stream == 0:
            send_y(2 * d)
        w_z_partner(stream, -d).start()
        if d < 4:
            w_z(stream, 3 + d).wait_recv()
            if d < 3:
                w_z(stream, 4 + d).start()
            if stream == 0:
                send_y(2 * d + 1)
            w_z_partner(stream, d).start()

    def across(*slots):
        for i in slots:
            w_y(i, True).wait_recv()
            if i == 0:
                w_z(2, 0).start()
                w_z(2, 4).start()
            w_y_partner(i).start()

    events = {
        0: [
            lambda: text_first(),
            lambda: across(0),
            lambda: ring(0, 1),
            lambda: ring(1, 1),
            lambda: text_second(),
            lambda: ring(2, 1),
            lambda: text_partner().wait_recv(),
        ],
        1: [lambda: ring(0, 2), lambda: across(1, 2, 3)],
        2: [lambda: ring(1, 2)],
        3: [lambda: ring(2, 2)],
        4: [lambda: ring(0, 3), lambda: across(4, 5)],
        5: [lambda: ring(1, 3)],
        6: [lambda: ring(2, 3)],
        7: [lambda: ring(0, 4), lambda: across(6, 7)],
        8: [lambda: ring(1, 4)],
        9: [lambda: project_own(0), lambda: ring(2, 4)],
        10: [lambda: project_own(1), lambda: across(8)],
    }
    own_side = pl.ds(pl.multiple_of(y_lo * SIDE, SIDE), SIDE)
    other_side = pl.ds(pl.multiple_of((1 - y_lo) * SIDE, SIDE), SIDE)

    def project_own(part):
        for d in (-4, -3, -2, -1, 1, 2, 3):
            w_z_partner(part, d).wait_recv()

        def column(j, _):
            cols = pl.ds(pl.multiple_of(j * OUT_COLS, OUT_COLS), OUT_COLS)
            acc[:, cols] = jnp.dot(
                att[:, own_side], wfull[own_side, cols], preferred_element_type=jnp.float32
            )
            return 0

        lax.fori_loop(part * BLOCKS, part * BLOCKS + BLOCKS, column, 0)

    def step(h, _):
        for at, actions in events.items():

            @pl.when(h == at)
            def _():
                for action in actions:
                    action()

        @pl.when(h < HEADS - 2)
        def _():
            kv_near(head_of(h + 2)).start()

        head = head_of(h)
        kv_near(head).wait_recv()

        @pl.when(has_far)
        def _():
            kv_far(head).wait_recv()

        attend_head(head, q, kvb, txt, mask, att)

        return 0

    lax.fori_loop(0, HEADS, step, 0)

    def copy_out(j):
        cols = pl.ds(pl.multiple_of(j * OUT_COLS, OUT_COLS), OUT_COLS)
        return pltpu.make_async_copy(res.at[:, cols], out_hbm.at[:, cols], out_sem.at[j])

    def finish(j, _):
        cols = pl.ds(pl.multiple_of(j * OUT_COLS, OUT_COLS), OUT_COLS)
        projected = acc[:, cols] + jnp.dot(
            att[:, other_side], wfull[other_side, cols], preferred_element_type=jnp.float32
        )
        result = res[:, cols].astype(jnp.float32) + gate[:, cols] * (projected + bias[:, cols])
        res[:, cols] = result.astype(jnp.bfloat16)
        copy_out(j).start()
        return 0

    w_y_partner(0).wait_recv()
    for d in (-4, -3, -2, -1, 1, 2, 3):
        w_z_partner(2, d).wait_recv()
    lax.fori_loop(BLOCKS, 2 * BLOCKS, finish, 0)
    for i in range(1, 9):
        w_y_partner(i).wait_recv()
    lax.fori_loop(0, BLOCKS, finish, 0)

    text_y().wait_send()
    for i in range(3):
        text_x(i, False).wait_send()
        text_x(i, True).wait_send()
    text_partner().wait_send()
    for stream in range(3):
        for slot in range(7):
            w_z(stream, slot).wait_send()
        for d in (-4, -3, -2, -1, 1, 2, 3):
            w_z_partner(stream, d).wait_send()
    for i in range(9):
        w_y_partner(i).wait_send()

    @pl.when(up_y)
    def _():
        for i in range(9):
            w_y(i, True).wait_send()

    @pl.when(down_y)
    def _():
        for i in range(9):
            w_y(i, False).wait_send()


    def sent(h, _):
        kv_near(h).wait_send()

        @pl.when(has_far)
        def _():
            kv_far(h).wait_send()

        return 0

    lax.fori_loop(0, HEADS, sent, 0)
    lax.fori_loop(0, D // OUT_COLS, lambda j, _: (copy_out(j).wait(), 0)[1], 0)


def on_device(
    queries, key_value, text_kv, residual, gate, bias, proj_weight, block_list, block_count
):
    hbm = pl.BlockSpec(memory_space=pl.ANY)
    vmem = pl.BlockSpec(memory_space=pltpu.VMEM)
    smem = pl.BlockSpec(memory_space=pltpu.SMEM)
    dma = pltpu.SemaphoreType.DMA
    result = pl.pallas_call(
        kernel,
        out_shape=jax.ShapeDtypeStruct((ROWS, D), jnp.bfloat16),
        in_specs=[hbm, hbm, hbm, hbm, vmem, vmem, hbm, smem, smem],
        out_specs=hbm,
        scratch_shapes=[
            pltpu.VMEM((ROWS, HD), jnp.bfloat16),
            pltpu.VMEM((3, 2, ROWS, HD), jnp.bfloat16),
            pltpu.VMEM((2, TXT, HD), jnp.bfloat16),
            pltpu.VMEM((HD, D), jnp.bfloat16),
            pltpu.VMEM((TPD, 3 * ROWS), jnp.float32),
            pltpu.VMEM((ROWS, HD), jnp.bfloat16),
            pltpu.VMEM((ROWS, D), jnp.float32),
            pltpu.VMEM((ROWS, D), jnp.bfloat16),
            dma((6,)),
            dma((D // OUT_COLS,)),
            dma((HEADS,)),
            dma((HEADS,)),
            dma((HEADS,)),
            dma((HEADS,)),
            dma((8,)),
            dma((8,)),
            dma((21,)),
            dma((21,)),
            dma((18,)),
            dma((9,)),
            dma((30,)),
            dma((30,)),
        ],
        compiler_params=pltpu.CompilerParams(
            collective_id=0, has_side_effects=True, vmem_limit_bytes=60 * 2**20
        ),
    )(
        queries[0],
        key_value[:, 0],
        text_kv[:, 0],
        residual[0],
        gate,
        bias[None],
        proj_weight,
        block_list,
        block_count,
    )
    return result[None]


def solution(mesh):
    placed = (
        P("prompt", "slab", None),
        P(None, "prompt", "slab", None),
        P(None, "prompt", "slab", None),
        P("prompt", "slab", None),
        P("prompt", None),
        P(),
        P("prompt", None),
        P("slab", None),
        P("slab"),
    )
    return jax.shard_map(
        on_device, mesh=mesh, in_specs=placed, out_specs=P("prompt", "slab", None), check_vma=False
    )
```

```python
import functools

import jax
import jax.numpy as jnp
from jax import lax
from jax.experimental import pallas as pl
from jax.experimental.pallas import tpu as pltpu
from jax.sharding import PartitionSpec as P

MESH = pl.DeviceIdType.MESH
HEADS = 12
HDIM = 128
TILE = 128
TPD = 4
NB = 8
ROWS = 512
HD = 1536
D = 3072
TXT = 256
SHARD = 96
HALF = 48
BLOCK = 256
OUT_COLS = 512
BLOCKS = 3
SIDE = 768
PART = 1536
masked_score = -1e30
EXP2_SCALE = HDIM**-0.5 * 1.4426950408889634
CONTRACT_LAST = (((1,), (1,)), ((), ()))


def scores_of(rows, keys, start, mask, source):
    scores = lax.dot_general(rows, keys, CONTRACT_LAST, preferred_element_type=jnp.float32)
    tiles = []
    for t in range(BLOCK // TILE):
        at = start // TILE + t
        tiles.append(
            scores[t * TILE : (t + 1) * TILE]
            + mask[at : at + 1, source * ROWS : (source + 1) * ROWS]
        )
    return jnp.concatenate(tiles, 0)


def largest_of(parts):
    return functools.reduce(jnp.maximum, [jnp.max(part, axis=1, keepdims=True) for part in parts])


def weigh(part, shift, values):
    weights = jnp.exp2(part * EXP2_SCALE - shift)
    weighted = jnp.dot(weights.astype(jnp.bfloat16), values, preferred_element_type=jnp.float32)
    return jnp.sum(weights, axis=1, keepdims=True), weighted


def columns_of(head):
    return pl.ds(pl.multiple_of(head * HDIM, HDIM), HDIM)


def attend_head(head, q, kvb, txt, mask, att):
    col = columns_of(head)
    for start in range(0, ROWS, BLOCK):
        rows = q[pl.ds(start, BLOCK), col]
        parts = [scores_of(rows, kvb[i, 0, :, col], start, mask, i) for i in range(3)]
        parts.append(
            lax.dot_general(rows, txt[0, :, col], CONTRACT_LAST, preferred_element_type=jnp.float32)
        )
        shift = largest_of(parts) * EXP2_SCALE
        total, weighted = None, None
        for i, part in enumerate(parts):
            values = kvb[i, 1, :, col] if i < 3 else txt[1, :, col]
            part_total, part_weighted = weigh(part, shift, values)
            total = part_total if i == 0 else total + part_total
            weighted = part_weighted if i == 0 else weighted + part_weighted
        att[pl.ds(start, BLOCK), col] = (weighted / total).astype(jnp.bfloat16)


def kernel(
    q_hbm,
    kv_hbm,
    t_hbm,
    res_hbm,
    gate,
    bias,
    w_hbm,
    block_list,
    block_count,
    out,
    q,
    kvb,
    txt,
    wfull,
    mask,
    att,
    acc,
    res,
    local_sem,
    kvx_send,
    kvx_recv,
    kvc_send,
    kvc_recv,
    text_send,
    text_recv,
    wz_send,
    wz_recv,
    wy_send,
    wy_recv,
    wp_send,
    wp_recv,
):
    p, s = lax.axis_index("prompt"), lax.axis_index("slab")
    y_lo, z = p // 8, p % 8
    y_hi, x, c = s // 8, (s % 8) // 2, s % 2
    y = y_hi * 2 + y_lo

    def device(x, y, z, c):
        return {"prompt": (y % 2) * 8 + z, "slab": (y // 2) * 8 + x * 2 + c}

    partner = device(x, y, z, 1 - c)
    far = s - 1 + 2 * c
    has_far = (far >= 0) & (far < 16)
    far_device = {"prompt": p, "slab": jnp.clip(far, 0, 15)}
    along = 1 - 2 * c
    z_of = lambda k: lax.rem(z + along * k + 8, 8)
    z_next, z_prev = device(x, y, z_of(1), c), device(x, y, z_of(-1), c)
    y_next, y_prev = device(x, lax.rem(y + 1, 4), z, c), device(x, lax.rem(y + 3, 4), z, c)
    both_y = ((x == 0) & (y_hi == 1)) | ((x == 3) & (y_hi == 0))
    inner = (x == 1) | (x == 2)
    up_y, down_y = both_y | (inner & (y_lo == 0)), both_y | (inner & (y_lo == 1))
    head_of = lambda i: lax.rem(i + y_lo * 6, HEADS)
    y_far = device(x, lax.rem(y + 2, 4), z, c)
    x_others = [device(lax.rem(x + dx, 4), y, z, c) for dx in (1, 2, 3)]

    barrier = pltpu.get_barrier_semaphore()
    fixed = [partner, z_next, z_prev, y_next, y_prev, y_far] + x_others
    for target in fixed:
        pl.semaphore_signal(barrier, inc=1, device_id=target, device_id_type=MESH)

    @pl.when(has_far)
    def _():
        pl.semaphore_signal(barrier, inc=1, device_id=far_device, device_id_type=MESH)

    text_own = pl.ds(pl.multiple_of(((c * 2 + y_hi) * 4 + x) * 16, 16), 16)
    text_over = pl.ds(pl.multiple_of(((c * 2 + 1 - y_hi) * 4 + x) * 16, 16), 16)
    copy_q = pltpu.make_async_copy(q_hbm, q, local_sem.at[0])
    copy_kv = pltpu.make_async_copy(kv_hbm, kvb.at[0], local_sem.at[1])
    copy_text = pltpu.make_async_copy(t_hbm, txt.at[:, text_own, :], local_sem.at[2])
    copy_w = pltpu.make_async_copy(
        w_hbm, wfull.at[pl.ds(pl.multiple_of(p * SHARD, SHARD), SHARD)], local_sem.at[3]
    )
    copy_res = pltpu.make_async_copy(res_hbm, res, local_sem.at[4])
    copy_edge = pltpu.make_async_copy(kv_hbm, kvb.at[2], local_sem.at[5])
    for copy in (copy_text, copy_kv, copy_q, copy_w, copy_res):
        copy.start()

    @pl.when(jnp.logical_not(has_far))
    def _():
        copy_edge.start()

    lane = lax.broadcasted_iota(jnp.int32, (1, 3 * ROWS), 1)
    slab_of = jnp.where(lane < ROWS, s, jnp.where(lane < 2 * ROWS, s + 1 - 2 * c, far))
    tile_of = slab_of * TPD + lax.rem(lane, ROWS) // TILE
    for t in range(TPD):
        member = None
        for n in range(NB):
            listed = jnp.where(n < block_count[t], block_list[t, n], -1000)
            match = tile_of == listed
            member = match if n == 0 else member | match
        mask[t : t + 1, :] = jnp.where(member, 0.0, masked_score)

    pl.semaphore_wait(barrier, len(fixed) + has_far.astype(jnp.int32))

    def remote(src, dst, send_sem, recv_sem, to):
        return pltpu.make_async_remote_copy(
            src_ref=src,
            dst_ref=dst,
            send_sem=send_sem,
            recv_sem=recv_sem,
            device_id=to,
            device_id_type=MESH,
        )

    text_half = pl.ds(pl.multiple_of(c * 128, 128), 128)

    def text_y():
        return remote(t_hbm, txt.at[:, text_own, :], text_send.at[0], text_recv.at[0], y_far)

    def text_x(i, over):
        rows, at = (text_over, 4 + i) if over else (text_own, 1 + i)
        src = txt.at[:, rows, :] if over else t_hbm
        return remote(src, txt.at[:, rows, :], text_send.at[at], text_recv.at[at], x_others[i])

    def text_partner():
        block = txt.at[:, text_half, :]
        return remote(block, block, text_send.at[7], text_recv.at[7], partner)

    def w_block(side, z_at, core, part):
        start = (side * 8 + z_at) * SHARD + core * HALF
        return wfull.at[pl.ds(pl.multiple_of(start, 16), HALF), pl.ds(part * PART, PART)]

    def w_own(part):
        return w_hbm.at[pl.ds(pl.multiple_of(c * HALF, 16), HALF), pl.ds(part * PART, PART)]

    sides, parts = (y_lo, y_lo, 1 - y_lo), (0, 1, 1)

    def w_z(stream, slot):
        offset = -slot if slot < 4 else slot - 4
        dst = w_block(sides[stream], z_of(offset), c, parts[stream])
        src = w_own(parts[stream]) if stream < 2 and offset == 0 else dst
        at = stream * 7 + slot
        return remote(src, dst, wz_send.at[at], wz_recv.at[at], z_next if slot < 4 else z_prev)

    def w_z_partner(stream, offset):
        block = w_block(sides[stream], z_of(offset), c, parts[stream])
        at = stream * 7 + (-offset - 1 if offset < 0 else 3 + offset)
        return remote(block, block, wp_send.at[at], wp_recv.at[at], partner)

    across_offsets = [0, 0, -1, 1, -2, 2, -3, 3, -4]

    def w_y(i, up):
        part = 1 if i == 0 else 0
        dst = w_block(y_lo, z_of(across_offsets[i]), c, part)
        src = w_own(part) if i < 2 else dst
        at = i if up else 9 + i
        return remote(src, dst, wy_send.at[at], wy_recv.at[i], y_next if up else y_prev)

    def w_y_partner(i):
        block = w_block(1 - y_lo, z_of(across_offsets[i]), c, 1 if i == 0 else 0)
        return remote(block, block, wp_send.at[21 + i], wp_recv.at[21 + i], partner)

    def send_y(i):
        pl.when(up_y)(lambda: w_y(i, True).start())
        pl.when(down_y)(lambda: w_y(i, False).start())

    def kv_cols(h):
        if isinstance(h, int):
            return pl.ds(h * HDIM, HDIM)
        return pl.ds(pl.multiple_of(h * HDIM, HDIM), HDIM)

    def kv_far(h):
        return remote(
            kv_hbm.at[:, :, kv_cols(h)],
            kvb.at[2, :, :, kv_cols(h)],
            kvx_send.at[h],
            kvx_recv.at[h],
            far_device,
        )

    def kv_near(h):
        return remote(
            kv_hbm.at[:, :, kv_cols(h)],
            kvb.at[1, :, :, kv_cols(h)],
            kvc_send.at[h],
            kvc_recv.at[h],
            partner,
        )

    def send_far(first, last):
        @pl.when(has_far)
        def _():
            for i in range(first, last):
                kv_far(head_of(i)).start()

    text_y().start()
    w_z(0, 0).start()
    w_z(0, 4).start()
    send_y(0)
    for i in range(3):
        text_x(i, False).start()
    send_far(0, 1)
    w_z(1, 0).start()
    w_z(1, 4).start()
    send_y(1)
    kv_near(head_of(0)).start()
    kv_near(head_of(1)).start()

    copy_text.wait()
    copy_kv.wait()
    copy_q.wait()
    copy_w.wait()
    copy_res.wait()

    @pl.when(jnp.logical_not(has_far))
    def _():
        copy_edge.wait()

    def text_first():
        text_y().wait_recv()
        for i in range(3):
            text_x(i, True).start()
        send_far(1, HEADS)

    def text_second():
        for i in range(3):
            text_x(i, False).wait_recv()
            text_x(i, True).wait_recv()
        text_partner().start()

    def ring(stream, d):
        w_z(stream, d - 1).wait_recv()
        if d < 4:
            w_z(stream, d).start()
        if stream == 0:
            send_y(2 * d)
        w_z_partner(stream, -d).start()
        if d < 4:
            w_z(stream, 3 + d).wait_recv()
            if d < 3:
                w_z(stream, 4 + d).start()
            if stream == 0:
                send_y(2 * d + 1)
            w_z_partner(stream, d).start()

    def across(*slots):
        for i in slots:
            w_y(i, True).wait_recv()
            if i == 0:
                w_z(2, 0).start()
                w_z(2, 4).start()
            w_y_partner(i).start()

    events = {
        0: [
            lambda: text_first(),
            lambda: across(0),
            lambda: ring(0, 1),
            lambda: ring(1, 1),
            lambda: text_second(),
            lambda: ring(2, 1),
            lambda: text_partner().wait_recv(),
        ],
        1: [lambda: ring(0, 2), lambda: across(1, 2, 3)],
        2: [lambda: ring(1, 2)],
        3: [lambda: ring(2, 2)],
        4: [lambda: ring(0, 3), lambda: across(4, 5)],
        5: [lambda: ring(1, 3)],
        6: [lambda: ring(2, 3)],
        7: [lambda: ring(0, 4), lambda: across(6, 7)],
        8: [lambda: ring(1, 4)],
        9: [lambda: ring(2, 4), lambda: project_own(0)],
        10: [lambda: across(8)],
        11: [lambda: project_own(1)],
    }
    own_side = pl.ds(pl.multiple_of(y_lo * SIDE, SIDE), SIDE)
    other_side = pl.ds(pl.multiple_of((1 - y_lo) * SIDE, SIDE), SIDE)

    def project_own(part):
        for d in (-4, -3, -2, -1, 1, 2, 3):
            w_z_partner(part, d).wait_recv()

        def column(j, _):
            cols = pl.ds(pl.multiple_of(j * OUT_COLS, OUT_COLS), OUT_COLS)
            projected = jnp.dot(
                att[:, own_side], wfull[own_side, cols], preferred_element_type=jnp.float32
            )
            acc[:, cols] = res[:, cols].astype(jnp.float32) + gate[:, cols] * (
                projected + bias[:, cols]
            )
            return 0

        lax.fori_loop(part * BLOCKS, part * BLOCKS + BLOCKS, column, 0)

    def step(h, _):
        for at, actions in events.items():

            @pl.when(h == at)
            def _():
                for action in actions:
                    action()

        @pl.when(h < HEADS - 2)
        def _():
            kv_near(head_of(h + 2)).start()

        head = head_of(h)
        kv_near(head).wait_recv()

        @pl.when(has_far)
        def _():
            kv_far(head).wait_recv()

        attend_head(head, q, kvb, txt, mask, att)
        return 0

    lax.fori_loop(0, HEADS, step, 0)

    def finish(j, _):
        cols = pl.ds(pl.multiple_of(j * OUT_COLS, OUT_COLS), OUT_COLS)
        projected = jnp.dot(
            att[:, other_side], wfull[other_side, cols], preferred_element_type=jnp.float32
        )
        result = acc[:, cols] + gate[:, cols] * projected
        out[:, cols] = result.astype(jnp.bfloat16)
        return 0

    w_y_partner(0).wait_recv()
    for d in (-4, -3, -2, -1, 1, 2, 3):
        w_z_partner(2, d).wait_recv()
    lax.fori_loop(BLOCKS, 2 * BLOCKS, finish, 0)
    for i in range(1, 9):
        w_y_partner(i).wait_recv()
    lax.fori_loop(0, BLOCKS, finish, 0)

    text_y().wait_send()
    for i in range(3):
        text_x(i, False).wait_send()
        text_x(i, True).wait_send()
    text_partner().wait_send()
    for stream in range(3):
        for slot in range(7):
            w_z(stream, slot).wait_send()
        for d in (-4, -3, -2, -1, 1, 2, 3):
            w_z_partner(stream, d).wait_send()
    for i in range(9):
        w_y_partner(i).wait_send()

    @pl.when(up_y)
    def _():
        for i in range(9):
            w_y(i, True).wait_send()

    @pl.when(down_y)
    def _():
        for i in range(9):
            w_y(i, False).wait_send()


    def sent(h, _):
        kv_near(h).wait_send()

        @pl.when(has_far)
        def _():
            kv_far(h).wait_send()

        return 0

    lax.fori_loop(0, HEADS, sent, 0)


def on_device(
    queries, key_value, text_kv, residual, gate, bias, proj_weight, block_list, block_count
):
    hbm = pl.BlockSpec(memory_space=pl.ANY)
    vmem = pl.BlockSpec(memory_space=pltpu.VMEM)
    smem = pl.BlockSpec(memory_space=pltpu.SMEM)
    dma = pltpu.SemaphoreType.DMA
    result = pl.pallas_call(
        kernel,
        out_shape=pltpu.VMEM((ROWS, D), jnp.bfloat16),
        in_specs=[hbm, hbm, hbm, hbm, vmem, vmem, hbm, smem, smem],
        out_specs=vmem,
        scratch_shapes=[
            pltpu.VMEM((ROWS, HD), jnp.bfloat16),
            pltpu.VMEM((3, 2, ROWS, HD), jnp.bfloat16),
            pltpu.VMEM((2, TXT, HD), jnp.bfloat16),
            pltpu.VMEM((HD, D), jnp.bfloat16),
            pltpu.VMEM((TPD, 3 * ROWS), jnp.float32),
            pltpu.VMEM((ROWS, HD), jnp.bfloat16),
            pltpu.VMEM((ROWS, D), jnp.float32),
            pltpu.VMEM((ROWS, D), jnp.bfloat16),
            dma((6,)),
            dma((HEADS,)),
            dma((HEADS,)),
            dma((HEADS,)),
            dma((HEADS,)),
            dma((8,)),
            dma((8,)),
            dma((21,)),
            dma((21,)),
            dma((18,)),
            dma((9,)),
            dma((30,)),
            dma((30,)),
        ],
        compiler_params=pltpu.CompilerParams(
            collective_id=0, has_side_effects=True, vmem_limit_bytes=58 * 2**20
        ),
    )(
        queries[0],
        key_value[:, 0],
        text_kv[:, 0],
        residual[0],
        gate,
        bias[None],
        proj_weight,
        block_list,
        block_count,
    )
    return result[None]


def solution(mesh):
    placed = (
        P("prompt", "slab", None),
        P(None, "prompt", "slab", None),
        P(None, "prompt", "slab", None),
        P("prompt", "slab", None),
        P("prompt", None),
        P(),
        P("prompt", None),
        P("slab", None),
        P("slab"),
    )
    return jax.shard_map(
        on_device, mesh=mesh, in_specs=placed, out_specs=P("prompt", "slab", None), check_vma=False
    )
```

```python
import functools

import jax
import jax.numpy as jnp
from jax import lax
from jax.experimental import pallas as pl
from jax.experimental.pallas import tpu as pltpu
from jax.sharding import PartitionSpec as P

MESH = pl.DeviceIdType.MESH
HEADS = 12
HDIM = 128
TILE = 128
TPD = 4
NB = 8
ROWS = 512
HD = 1536
D = 3072
TXT = 256
SHARD = 96
HALF = 48
BLOCK = 256
OUT_COLS = 1536
BLOCKS = 1
SIDE = 768
PART = 1536
masked_score = -1e30
EXP2_SCALE = HDIM**-0.5 * 1.4426950408889634
CONTRACT_LAST = (((1,), (1,)), ((), ()))


def scores_of(rows, keys, start, mask, source):
    scores = lax.dot_general(rows, keys, CONTRACT_LAST, preferred_element_type=jnp.float32)
    tiles = []
    for t in range(BLOCK // TILE):
        at = start // TILE + t
        tiles.append(
            scores[t * TILE : (t + 1) * TILE]
            + mask[at : at + 1, source * ROWS : (source + 1) * ROWS]
        )
    return jnp.concatenate(tiles, 0)


def largest_of(parts):
    return functools.reduce(jnp.maximum, [jnp.max(part, axis=1, keepdims=True) for part in parts])


def weigh(part, shift, values):
    weights = jnp.exp2(part * EXP2_SCALE - shift)
    weighted = jnp.dot(weights.astype(jnp.bfloat16), values, preferred_element_type=jnp.float32)
    return jnp.sum(weights, axis=1, keepdims=True), weighted


def columns_of(head):
    return pl.ds(pl.multiple_of(head * HDIM, HDIM), HDIM)


def attend_head(head, q, kvb, txt, mask, att):
    col = columns_of(head)
    for start in range(0, ROWS, BLOCK):
        rows = q[pl.ds(start, BLOCK), col]
        parts = [scores_of(rows, kvb[i, 0, :, col], start, mask, i) for i in range(3)]
        parts.append(
            lax.dot_general(rows, txt[0, :, col], CONTRACT_LAST, preferred_element_type=jnp.float32)
        )
        shift = largest_of(parts) * EXP2_SCALE
        total, weighted = None, None
        for i, part in enumerate(parts):
            values = kvb[i, 1, :, col] if i < 3 else txt[1, :, col]
            part_total, part_weighted = weigh(part, shift, values)
            total = part_total if i == 0 else total + part_total
            weighted = part_weighted if i == 0 else weighted + part_weighted
        att[pl.ds(start, BLOCK), col] = (weighted / total).astype(jnp.bfloat16)


def attend_near(head, q, kvb, txt, mask):
    col = columns_of(head)
    states = []
    for start in range(0, ROWS, BLOCK):
        rows = q[pl.ds(start, BLOCK), col]
        parts = [scores_of(rows, kvb[i, 0, :, col], start, mask, i) for i in range(2)]
        parts.append(
            lax.dot_general(rows, txt[0, :, col], CONTRACT_LAST, preferred_element_type=jnp.float32)
        )
        shift = largest_of(parts) * EXP2_SCALE
        total, weighted = weigh(parts[2], shift, txt[1, :, col])
        for i in range(2):
            part_total, part_weighted = weigh(parts[i], shift, kvb[i, 1, :, col])
            total, weighted = total + part_total, weighted + part_weighted
        states.append((shift, total, weighted))
    return states


def attend_far(head, q, kvb, mask, att, states):
    col = columns_of(head)
    for start, (near_shift, total, weighted) in zip(range(0, ROWS, BLOCK), states):
        rows = q[pl.ds(start, BLOCK), col]
        scores = scores_of(rows, kvb[2, 0, :, col], start, mask, 2)
        shift = jnp.maximum(near_shift, largest_of([scores]) * EXP2_SCALE)
        scale = jnp.exp2(near_shift - shift)
        far_total, far_weighted = weigh(scores, shift, kvb[2, 1, :, col])
        total = total * scale + far_total
        att[pl.ds(start, BLOCK), col] = ((weighted * scale + far_weighted) / total).astype(
            jnp.bfloat16
        )


def kernel(
    q_hbm,
    kv_hbm,
    t_hbm,
    res_hbm,
    gate,
    bias,
    w_hbm,
    block_list,
    block_count,
    out,
    q,
    kvb,
    txt,
    wfull,
    mask,
    att,
    acc,
    res,
    local_sem,
    kvx_send,
    kvx_recv,
    kvc_send,
    kvc_recv,
    text_send,
    text_recv,
    wz_send,
    wz_recv,
    wy_send,
    wy_recv,
    wp_send,
    wp_recv,
):
    p, s = lax.axis_index("prompt"), lax.axis_index("slab")
    y_lo, z = p // 8, p % 8
    y_hi, x, c = s // 8, (s % 8) // 2, s % 2
    y = y_hi * 2 + y_lo

    def device(x, y, z, c):
        return {"prompt": (y % 2) * 8 + z, "slab": (y // 2) * 8 + x * 2 + c}

    partner = device(x, y, z, 1 - c)
    far = s - 1 + 2 * c
    has_far = (far >= 0) & (far < 16)
    far_device = {"prompt": p, "slab": jnp.clip(far, 0, 15)}
    along = 1 - 2 * c
    z_of = lambda k: lax.rem(z + along * k + 8, 8)
    z_next, z_prev = device(x, y, z_of(1), c), device(x, y, z_of(-1), c)
    y_next, y_prev = device(x, lax.rem(y + 1, 4), z, c), device(x, lax.rem(y + 3, 4), z, c)
    both_y = ((x == 0) & (y_hi == 1)) | ((x == 3) & (y_hi == 0))
    inner = (x == 1) | (x == 2)
    up_y, down_y = both_y | (inner & (y_lo == 0)), both_y | (inner & (y_lo == 1))
    head_of = lambda i: lax.rem(i + y_lo * 6, HEADS)
    y_far = device(x, lax.rem(y + 2, 4), z, c)
    x_others = [device(lax.rem(x + dx, 4), y, z, c) for dx in (1, 2, 3)]

    barrier = pltpu.get_barrier_semaphore()
    fixed = [partner, z_next, z_prev, y_next, y_prev, y_far] + x_others
    for target in fixed:
        pl.semaphore_signal(barrier, inc=1, device_id=target, device_id_type=MESH)

    @pl.when(has_far)
    def _():
        pl.semaphore_signal(barrier, inc=1, device_id=far_device, device_id_type=MESH)

    text_own = pl.ds(pl.multiple_of(((c * 2 + y_hi) * 4 + x) * 16, 16), 16)
    text_over = pl.ds(pl.multiple_of(((c * 2 + 1 - y_hi) * 4 + x) * 16, 16), 16)
    copy_q = pltpu.make_async_copy(q_hbm, q, local_sem.at[0])
    copy_kv = pltpu.make_async_copy(kv_hbm, kvb.at[0], local_sem.at[1])
    copy_text = pltpu.make_async_copy(t_hbm, txt.at[:, text_own, :], local_sem.at[2])
    copy_w = pltpu.make_async_copy(
        w_hbm, wfull.at[pl.ds(pl.multiple_of(p * SHARD, SHARD), SHARD)], local_sem.at[3]
    )
    copy_res = pltpu.make_async_copy(res_hbm, res, local_sem.at[4])
    copy_edge = pltpu.make_async_copy(kv_hbm, kvb.at[2], local_sem.at[5])
    for copy in (copy_text, copy_kv, copy_q, copy_w, copy_res):
        copy.start()

    @pl.when(jnp.logical_not(has_far))
    def _():
        copy_edge.start()

    lane = lax.broadcasted_iota(jnp.int32, (1, 3 * ROWS), 1)
    slab_of = jnp.where(lane < ROWS, s, jnp.where(lane < 2 * ROWS, s + 1 - 2 * c, far))
    tile_of = slab_of * TPD + lax.rem(lane, ROWS) // TILE
    for t in range(TPD):
        member = None
        for n in range(NB):
            listed = jnp.where(n < block_count[t], block_list[t, n], -1000)
            match = tile_of == listed
            member = match if n == 0 else member | match
        mask[t : t + 1, :] = jnp.where(member, 0.0, masked_score)

    pl.semaphore_wait(barrier, len(fixed) + has_far.astype(jnp.int32))

    def remote(src, dst, send_sem, recv_sem, to):
        return pltpu.make_async_remote_copy(
            src_ref=src,
            dst_ref=dst,
            send_sem=send_sem,
            recv_sem=recv_sem,
            device_id=to,
            device_id_type=MESH,
        )

    text_half = pl.ds(pl.multiple_of(c * 128, 128), 128)

    def text_y():
        return remote(t_hbm, txt.at[:, text_own, :], text_send.at[0], text_recv.at[0], y_far)

    def text_x(i, over):
        rows, at = (text_over, 4 + i) if over else (text_own, 1 + i)
        src = txt.at[:, rows, :] if over else t_hbm
        return remote(src, txt.at[:, rows, :], text_send.at[at], text_recv.at[at], x_others[i])

    def text_partner():
        block = txt.at[:, text_half, :]
        return remote(block, block, text_send.at[7], text_recv.at[7], partner)

    def w_block(side, z_at, core, part):
        start = (side * 8 + z_at) * SHARD + core * HALF
        return wfull.at[pl.ds(pl.multiple_of(start, 16), HALF), pl.ds(part * PART, PART)]

    def w_own(part):
        return w_hbm.at[pl.ds(pl.multiple_of(c * HALF, 16), HALF), pl.ds(part * PART, PART)]

    sides, parts = (y_lo, y_lo, 1 - y_lo), (0, 1, 1)

    def w_z(stream, slot):
        offset = -slot if slot < 4 else slot - 4
        dst = w_block(sides[stream], z_of(offset), c, parts[stream])
        src = w_own(parts[stream]) if stream < 2 and offset == 0 else dst
        at = stream * 7 + slot
        return remote(src, dst, wz_send.at[at], wz_recv.at[at], z_next if slot < 4 else z_prev)

    def w_z_partner(stream, offset):
        block = w_block(sides[stream], z_of(offset), c, parts[stream])
        at = stream * 7 + (-offset - 1 if offset < 0 else 3 + offset)
        return remote(block, block, wp_send.at[at], wp_recv.at[at], partner)

    across_offsets = [0, 0, -1, 1, -2, 2, -3, 3, -4]

    def w_y(i, up):
        part = 1 if i == 0 else 0
        dst = w_block(y_lo, z_of(across_offsets[i]), c, part)
        src = w_own(part) if i < 2 else dst
        at = i if up else 9 + i
        return remote(src, dst, wy_send.at[at], wy_recv.at[i], y_next if up else y_prev)

    def w_y_partner(i):
        block = w_block(1 - y_lo, z_of(across_offsets[i]), c, 1 if i == 0 else 0)
        return remote(block, block, wp_send.at[21 + i], wp_recv.at[21 + i], partner)

    def send_y(i):
        pl.when(up_y)(lambda: w_y(i, True).start())
        pl.when(down_y)(lambda: w_y(i, False).start())

    def kv_cols(h):
        if isinstance(h, int):
            return pl.ds(h * HDIM, HDIM)
        return pl.ds(pl.multiple_of(h * HDIM, HDIM), HDIM)

    def kv_far(h):
        return remote(
            kv_hbm.at[:, :, kv_cols(h)],
            kvb.at[2, :, :, kv_cols(h)],
            kvx_send.at[h],
            kvx_recv.at[h],
            far_device,
        )

    def kv_near(h):
        return remote(
            kv_hbm.at[:, :, kv_cols(h)],
            kvb.at[1, :, :, kv_cols(h)],
            kvc_send.at[h],
            kvc_recv.at[h],
            partner,
        )

    def send_far(first, last):
        @pl.when(has_far)
        def _():
            for i in range(first, last):
                kv_far(head_of(i)).start()

    text_y().start()
    w_z(0, 0).start()
    w_z(0, 4).start()
    send_y(0)
    for i in range(3):
        text_x(i, False).start()
    send_far(0, 1)
    w_z(1, 0).start()
    w_z(1, 4).start()
    send_y(1)
    kv_near(head_of(0)).start()
    kv_near(head_of(1)).start()

    copy_text.wait()
    copy_kv.wait()
    copy_q.wait()
    copy_w.wait()
    copy_res.wait()

    @pl.when(jnp.logical_not(has_far))
    def _():
        copy_edge.wait()

    def text_first():
        text_y().wait_recv()
        for i in range(3):
            text_x(i, True).start()
        send_far(1, HEADS)

    def text_second():
        for i in range(3):
            text_x(i, False).wait_recv()
            text_x(i, True).wait_recv()
        text_partner().start()

    def ring(stream, d):
        w_z(stream, d - 1).wait_recv()
        if d < 4:
            w_z(stream, d).start()
        if stream == 0:
            send_y(2 * d)
        w_z_partner(stream, -d).start()
        if d < 4:
            w_z(stream, 3 + d).wait_recv()
            if d < 3:
                w_z(stream, 4 + d).start()
            if stream == 0:
                send_y(2 * d + 1)
            w_z_partner(stream, d).start()

    def across(*slots):
        for i in slots:
            w_y(i, True).wait_recv()
            if i == 0:
                w_z(2, 0).start()
                w_z(2, 4).start()
            w_y_partner(i).start()

    events = {
        0: [
            lambda: text_first(),
            lambda: across(0),
            lambda: ring(0, 1),
            lambda: ring(1, 1),
            lambda: text_second(),
            lambda: ring(2, 1),
            lambda: text_partner().wait_recv(),
        ],
        1: [lambda: ring(0, 2), lambda: across(1, 2, 3)],
        2: [lambda: ring(1, 2)],
        3: [lambda: ring(2, 2)],
        4: [lambda: ring(0, 3), lambda: across(4, 5)],
        5: [lambda: ring(1, 3)],
        6: [lambda: ring(2, 3)],
        7: [lambda: ring(0, 4), lambda: across(6, 7)],
        8: [lambda: ring(1, 4)],
        9: [lambda: ring(2, 4), lambda: project_own(0)],
        10: [lambda: across(8)],
    }
    own_side = pl.ds(pl.multiple_of(y_lo * SIDE, SIDE), SIDE)
    other_side = pl.ds(pl.multiple_of((1 - y_lo) * SIDE, SIDE), SIDE)

    def project_own(part):
        for d in (-4, -3, -2, -1, 1, 2, 3):
            w_z_partner(part, d).wait_recv()

        def column(j, _):
            cols = pl.ds(pl.multiple_of(j * OUT_COLS, OUT_COLS), OUT_COLS)
            projected = jnp.dot(
                att[:, own_side], wfull[own_side, cols], preferred_element_type=jnp.float32
            )
            acc[:, cols] = res[:, cols].astype(jnp.float32) + gate[:, cols] * (
                projected + bias[:, cols]
            )
            return 0

        lax.fori_loop(part * BLOCKS, part * BLOCKS + BLOCKS, column, 0)

    def step(h, _):
        for at, actions in events.items():

            @pl.when(h == at)
            def _():
                for action in actions:
                    action()

        @pl.when(h < HEADS - 2)
        def _():
            kv_near(head_of(h + 2)).start()

        head = head_of(h)
        kv_near(head).wait_recv()

        @pl.when(has_far)
        def _():
            kv_far(head).wait_recv()

        attend_head(head, q, kvb, txt, mask, att)
        return 0

    lax.fori_loop(0, HEADS - 1, step, 0)
    last = head_of(HEADS - 1)
    kv_near(last).wait_recv()
    states = attend_near(last, q, kvb, txt, mask)
    project_own(1)

    @pl.when(has_far)
    def _():
        kv_far(last).wait_recv()

    attend_far(last, q, kvb, mask, att, states)

    def finish(j, _):
        cols = pl.ds(pl.multiple_of(j * OUT_COLS, OUT_COLS), OUT_COLS)
        projected = jnp.dot(
            att[:, other_side], wfull[other_side, cols], preferred_element_type=jnp.float32
        )
        result = acc[:, cols] + gate[:, cols] * projected
        out[:, cols] = result.astype(jnp.bfloat16)
        return 0

    w_y_partner(0).wait_recv()
    for d in (-4, -3, -2, -1, 1, 2, 3):
        w_z_partner(2, d).wait_recv()
    lax.fori_loop(BLOCKS, 2 * BLOCKS, finish, 0)
    for i in range(1, 9):
        w_y_partner(i).wait_recv()
    lax.fori_loop(0, BLOCKS, finish, 0)

    text_y().wait_send()
    for i in range(3):
        text_x(i, False).wait_send()
        text_x(i, True).wait_send()
    text_partner().wait_send()
    for stream in range(3):
        for slot in range(7):
            w_z(stream, slot).wait_send()
        for d in (-4, -3, -2, -1, 1, 2, 3):
            w_z_partner(stream, d).wait_send()
    for i in range(9):
        w_y_partner(i).wait_send()

    @pl.when(up_y)
    def _():
        for i in range(9):
            w_y(i, True).wait_send()

    @pl.when(down_y)
    def _():
        for i in range(9):
            w_y(i, False).wait_send()


    def sent(h, _):
        kv_near(h).wait_send()

        @pl.when(has_far)
        def _():
            kv_far(h).wait_send()

        return 0

    lax.fori_loop(0, HEADS, sent, 0)


def on_device(
    queries, key_value, text_kv, residual, gate, bias, proj_weight, block_list, block_count
):
    hbm = pl.BlockSpec(memory_space=pl.ANY)
    vmem = pl.BlockSpec(memory_space=pltpu.VMEM)
    smem = pl.BlockSpec(memory_space=pltpu.SMEM)
    dma = pltpu.SemaphoreType.DMA
    result = pl.pallas_call(
        kernel,
        out_shape=pltpu.VMEM((ROWS, D), jnp.bfloat16),
        in_specs=[hbm, hbm, hbm, hbm, vmem, vmem, hbm, smem, smem],
        out_specs=vmem,
        scratch_shapes=[
            pltpu.VMEM((ROWS, HD), jnp.bfloat16),
            pltpu.VMEM((3, 2, ROWS, HD), jnp.bfloat16),
            pltpu.VMEM((2, TXT, HD), jnp.bfloat16),
            pltpu.VMEM((HD, D), jnp.bfloat16),
            pltpu.VMEM((TPD, 3 * ROWS), jnp.float32),
            pltpu.VMEM((ROWS, HD), jnp.bfloat16),
            pltpu.VMEM((ROWS, D), jnp.float32),
            pltpu.VMEM((ROWS, D), jnp.bfloat16),
            dma((6,)),
            dma((HEADS,)),
            dma((HEADS,)),
            dma((HEADS,)),
            dma((HEADS,)),
            dma((8,)),
            dma((8,)),
            dma((21,)),
            dma((21,)),
            dma((18,)),
            dma((9,)),
            dma((30,)),
            dma((30,)),
        ],
        compiler_params=pltpu.CompilerParams(
            collective_id=0, has_side_effects=True, vmem_limit_bytes=58 * 2**20
        ),
    )(
        queries[0],
        key_value[:, 0],
        text_kv[:, 0],
        residual[0],
        gate,
        bias[None],
        proj_weight,
        block_list,
        block_count,
    )
    return result[None]


def solution(mesh):
    placed = (
        P("prompt", "slab", None),
        P(None, "prompt", "slab", None),
        P(None, "prompt", "slab", None),
        P("prompt", "slab", None),
        P("prompt", None),
        P(),
        P("prompt", None),
        P("slab", None),
        P("slab"),
    )
    return jax.shard_map(
        on_device, mesh=mesh, in_specs=placed, out_specs=P("prompt", "slab", None), check_vma=False
    )
```
